32 devices in a mesh: dp: 2 (over x), inblk: 4 (over z), outcol: 4 (over y, core).
Axes of the slice: x: 2, y: 2, z: 4, core: 2. Of those that a mesh axis runs over, the one named last changes fastest.
Arguments:
- activations: bfloat16 [256, 8192], P('dp', ('inblk', 'outcol')), may hold values from -1.5 to 1.5
- cotangent: bfloat16 [256, 1024], P('dp', 'outcol'), may hold values from -6 to 6
- base_weight: bfloat16 [8192, 1024], P('inblk', 'outcol'), may hold values from -0.09375 to 0.09375
- skew_param: float32 [32, 256, 256], P(('inblk', 'outcol'), 'dp'), may hold values from -0.3125 to 0.3125
Outputs:
- grad_acts: bfloat16 [256, 8192], P('dp', ('inblk', 'outcol'))
- grad_skew: float32 [32, 256, 256], P(('inblk', 'outcol'), 'dp')
The draws below stay inside these ranges and needn't reach their ends.
All inputs are finite; a program needn't handle non-finite values.
Results may differ from the reference program's by a relative error of at most 0.0058.
Values may be sent and summed in bfloat16 or wider, within the bound.
A program may use at most 64 MiB of HBM per device.

```python
import jax
import jax.numpy as jnp
from jax import lax

D = 8192
KV = 1024
BLOCK = 256
TOKENS = 256
BLOCKS = 32


def strengthened(array, stream_key, source, target, parts, factor):
    owner, partner = [(jnp.arange(array.shape[axis_at]) // (array.shape[axis_at] // parts)).reshape([-1 if axis == axis_at else 1 for axis in range(array.ndim)]) for axis_at in (source, target)]
    chosen = jax.random.permutation(stream_key, parts)[partner]
    strong = (owner == chosen) | (owner == (partner + parts // 2) % parts)
    return jnp.where(strong, factor * array, array)


def level_of(own_key, shape, shards, smallest, high):
    def one(dim, parts):
        draws = jax.random.uniform(jax.random.fold_in(jax.random.fold_in(own_key, 6), dim), (parts,), jnp.float32, smallest / len(shards), high / len(shards))
        return jnp.repeat(jnp.exp(draws), shape[dim] // parts).reshape((-1,) + (1,) * (len(shape) - dim - 1))

    level = one(*shards[0])
    for cut in shards[1:]:
        level = level * one(*cut)
    return level


def bell_draw(stream_key, dims, scale, bound, cuts=(), kind=jnp.bfloat16):
    drawn = jax.random.normal(stream_key, dims, jnp.float32) * scale
    if len(cuts) > 0:
        drawn = level_of(stream_key, dims, cuts, -0.22, 0.18) * drawn
    return jnp.clip(drawn, min=-bound, max=bound).astype(kind)


def gaussian_with(own_key, shape, width, most, pieces, heavy, kind=jnp.bfloat16):
    result = width * jax.random.normal(own_key, shape, jnp.float32)
    if pieces:
        result = result * level_of(own_key, shape, pieces, -0.22, 0.18)
    return jnp.clip(strengthened(result, jax.random.fold_in(own_key, 3), *heavy), -most, most).astype(kind)


def setup_inputs(seed: int = 0) -> dict:
    key_of = jax.random.split(jax.random.key(seed), 5)
    activations = bell_draw(key_of[0], (TOKENS, D), 0.1, 1.5, ((0, 2), (1, 16)))
    cotangent = bell_draw(key_of[1], (TOKENS, KV), 1.0, 6.0, ((0, 2), (1, 4)))
    base_weight = gaussian_with(key_of[2], (D, KV), D ** -0.5, 0.09375, ((0, 4), (1, 4)), (1, 0, 4, 2.0))
    skew_param = bell_draw(key_of[3], (BLOCKS, BLOCK, BLOCK), 0.02, 0.3125, ((0, 16), (1, 2)), jnp.float32)
    return dict(activations=activations, cotangent=cotangent, base_weight=base_weight, skew_param=skew_param)


def high_product(left, right):
    return jnp.matmul(left, right, precision=lax.Precision.HIGHEST)


def power_list(skew_input):
    skew_mat = skew_input - jnp.swapaxes(skew_input, -1, -2)
    powers = [skew_mat]
    for degree in range(5):
        powers.append(high_product(powers[-1], skew_mat))
    return powers


def rotation_of(powers):
    block_width = powers[0].shape[-1]
    identity_mat = jnp.eye(block_width, dtype=jnp.float32)
    series = powers[0] + powers[1] + powers[2] + powers[3] + powers[4]
    return identity_mat + 2.0 * series + powers[5]


def chain_rule(grad_rot, powers):
    negated = [powers[degree] * ((-1.0) ** (degree + 1)) for degree in range(5)]
    partial_value = grad_rot
    running = 2.0 * grad_rot
    for degree in range(2, 7):
        partial_value = high_product(negated[0], partial_value) + high_product(grad_rot, negated[degree - 2])
        weight_factor = 2.0 if degree < 6 else 1.0
        running = running + weight_factor * partial_value
    return running - jnp.swapaxes(running, -1, -2)


def reference(activations, cotangent, base_weight, skew_param):
    features = jnp.dot(cotangent, base_weight.T, preferred_element_type=jnp.float32).astype(jnp.bfloat16)

    def per_block(block_idx):
        offset = (block_idx * BLOCK).astype(jnp.int32)
        inputs = lax.dynamic_slice_in_dim(activations, offset, BLOCK, 1)
        block_feat = lax.dynamic_slice_in_dim(features, offset, BLOCK, 1)
        skew_block = lax.dynamic_index_in_dim(skew_param, block_idx, 0, keepdims=False)
        powers = power_list(skew_block)
        rotation = rotation_of(powers).astype(jnp.bfloat16)
        grad_block = jnp.dot(block_feat, rotation.T, preferred_element_type=jnp.float32).astype(jnp.bfloat16)
        grad_rot = jnp.dot(inputs.T, block_feat, preferred_element_type=jnp.float32)
        return grad_block, chain_rule(grad_rot, powers)

    grad_blocks, grad_skew = lax.map(per_block, jnp.arange(D // BLOCK, dtype=jnp.int32))
    grad_acts = jnp.transpose(grad_blocks, (1, 0, 2)).reshape(TOKENS, D)
    return grad_acts, grad_skew
```

```python
import functools

import jax
import jax.numpy as jnp
from jax import lax
from jax.experimental import pallas as pl
from jax.experimental.pallas import tpu as pltpu
from jax.sharding import PartitionSpec as P

F32, BF16 = jnp.float32, jnp.bfloat16
MESH = pl.DeviceIdType.MESH


def mm(left, right):
    return jnp.dot(left, right, preferred_element_type=F32)


def halves(value):
    high = value.astype(BF16)
    return high, (value - high.astype(F32)).astype(BF16)


def mm3(left, right):
    return mm(left[0], right[0]) + (mm(left[0], right[1]) + mm(left[1], right[0]))


def kernel(n_dp, act_hbm, cot_hbm, w_hbm, skew_hbm, ga_ref, gs_ref,
           skew_own, skew_all, act_all, act_t, cot_v, w_v,
           s1_send, s1_recv, part, y_send, y_recv, feat, mats, dq_v,
           loc, skew_s, skew_r, act_s, act_r, s1_s, s1_r, y_s, y_r, f_s, f_r):
    me, out = lax.axis_index("dp"), lax.axis_index("outcol")
    side, core = lax.div(out, 2), lax.rem(out, 2)
    sib = side * 2 + 1 - core
    far = (1 - side) * 2 + core
    far_sib = (1 - side) * 2 + 1 - core
    tokens = cot_v.shape[0]
    rows = skew_own.shape[1]
    width = skew_own.shape[2]
    blocks = skew_own.shape[0]
    peers = [lax.rem(me + step, n_dp) for step in range(1, n_dp)]

    loads = [
        pltpu.make_async_copy(src, dst, loc.at[i])
        for i, (src, dst) in enumerate(
            ((cot_hbm, cot_v), (w_hbm, w_v), (skew_hbm, skew_own), (act_hbm, act_all.at[0]))
        )
    ]
    for load in loads:
        load.start()

    barrier = pltpu.get_barrier_semaphore()
    pl.semaphore_signal(barrier, inc=1, device_id={"outcol": sib}, device_id_type=MESH)
    pl.semaphore_signal(barrier, inc=1, device_id={"outcol": far}, device_id_type=MESH)
    for peer in peers:
        pl.semaphore_signal(barrier, inc=1, device_id={"dp": peer}, device_id_type=MESH)

    def partial_of(owner, block):
        start = pl.multiple_of((owner * blocks + block) * width, width)
        return lax.dot_general(
            cot_v[...], w_v[pl.ds(start, width), :], (((1,), (1,)), ((), ())),
            preferred_element_type=F32,
        )

    def remote(src, dst, send, recv, **where):
        return pltpu.make_async_remote_copy(
            src_ref=src, dst_ref=dst, send_sem=send, recv_sem=recv,
            device_id=where, device_id_type=MESH,
        )

    loads[0].wait()
    loads[1].wait()
    for block in range(blocks):
        s1_send[block, 0] = partial_of(sib, block).astype(BF16)
        s1_send[block, 1] = partial_of(far_sib, block).astype(BF16)
    loads[2].wait()
    skew_all[me] = skew_own[...].astype(skew_all.dtype)

    pl.semaphore_wait(barrier, 1 + n_dp)

    s1 = [remote(s1_send.at[b], s1_recv.at[b], s1_s.at[b], s1_r.at[b], outcol=sib)
          for b in range(blocks)]
    skews = [remote(skew_all.at[me], skew_all.at[me], skew_s.at[i], skew_r.at[i], dp=peer)
             for i, peer in enumerate(peers)]
    acts = [remote(act_hbm, act_all.at[i + 1], act_s.at[i], act_r.at[i], dp=peer)
            for i, peer in enumerate(peers)]
    for copy in s1 + skews + acts:
        copy.start()

    for block in range(blocks):
        part[block, 0] = partial_of(out, block)
        part[block, 1] = partial_of(far, block)

    sides = [remote(y_send.at[b], y_recv.at[b], y_s.at[b], y_r.at[b], outcol=far)
             for b in range(blocks)]
    for block in range(blocks):
        s1[block].wait_recv()
        y_send[block] = (part[block, 1] + s1_recv[block, 1].astype(F32)).astype(BF16)
        sides[block].start()
    feats = []
    for block in range(blocks):
        sides[block].wait_recv()
        total = part[block, 0] + s1_recv[block, 0].astype(F32) + y_recv[block].astype(F32)
        feat[block, 0] = total.astype(BF16)
        for i, peer in enumerate(peers):
            copy = remote(feat.at[block, 0], feat.at[block, i + 1],
                          f_s.at[block, i], f_r.at[block, i], dp=peer)
            copy.start()
            feats.append(copy)

    for copy in skews:
        copy.wait_recv()
    eye = (lax.broadcasted_iota(jnp.int32, (width, width), 0)
           == lax.broadcasted_iota(jnp.int32, (width, width), 1)).astype(F32)
    for block in range(blocks):
        given = skew_all[:, block].reshape(width, width).astype(F32)
        m1 = given.T - given
        m1_h = halves(m1)
        m2 = mm3(m1_h, m1_h)
        m2_h = halves(m2)
        m4 = mm3(m2_h, m2_h)
        k0 = 2.0 * m1 + m2
        k0_h = halves(k0)
        c2 = mm3(k0_h, m2_h)
        c4 = mm3(k0_h, halves(m4))
        n0 = m2 + m4
        rot_t = (eye + ((k0 + n0) + (c2 + c4))).astype(BF16)
        ga_ref[:, block * width:(block + 1) * width] = mm(feat[block, 0], rot_t).astype(BF16)
        mats[block, 0] = m1_h[0]
        mats[block, 1] = m2_h[0]
        mats[block, 2] = n0.astype(BF16)
        mats[block, 3] = k0_h[0]
        mats[block, 4] = (k0 + m2 + c2).astype(BF16)

    loads[3].wait()
    for copy in acts:
        copy.wait_recv()
    for slot in range(n_dp):
        act_t[:, slot * tokens:(slot + 1) * tokens] = act_all[slot].T

    for block in range(blocks):
        for copy in feats[block * (n_dp - 1):(block + 1) * (n_dp - 1)]:
            copy.wait_recv()
        grad = mm(act_t[block * width:(block + 1) * width, :],
                  feat[block].reshape(n_dp * tokens, width))
        grad_b = grad.astype(BF16)
        x = mm(mats[block, 0], grad_b) + mm(grad_b, mats[block, 0])
        x_b = x.astype(BF16)
        kx = (x + mm(mats[block, 3], x_b)).astype(BF16)
        dq = 2.0 * (grad + x) + mm(mats[block, 4], x_b)
        dq = dq + mm((2.0 * grad + x).astype(BF16), mats[block, 2]) + mm(kx, mats[block, 1])
        dq_v[block] = dq - dq.T
        gs_ref[block] = dq_v[block, pl.ds(pl.multiple_of(me * rows, rows), rows), :]

    for copy in s1 + skews + acts + sides + feats:
        copy.wait_send()


def body(n_dp, activations, cotangent, base_weight, skew_param):
    tokens, own = activations.shape
    blocks, rows, width = skew_param.shape
    wire = BF16 if rows % 16 == 0 else F32
    dma = pltpu.SemaphoreType.DMA
    return tuple(pl.pallas_call(
        functools.partial(kernel, n_dp),
        out_shape=(jax.ShapeDtypeStruct((tokens, own), BF16),
                   jax.ShapeDtypeStruct((blocks, rows, width), F32)),
        in_specs=[pl.BlockSpec(memory_space=pl.ANY)] * 4,
        out_specs=[pl.BlockSpec(memory_space=pltpu.VMEM)] * 2,
        scratch_shapes=[
            pltpu.VMEM((blocks, rows, width), F32),
            pltpu.VMEM((n_dp, blocks, rows, width), wire),
            pltpu.VMEM((n_dp, tokens, own), BF16),
            pltpu.VMEM((own, n_dp * tokens), BF16),
            pltpu.VMEM(cotangent.shape, BF16),
            pltpu.VMEM(base_weight.shape, BF16),
            pltpu.VMEM((blocks, 2, tokens, width), BF16),
            pltpu.VMEM((blocks, 2, tokens, width), BF16),
            pltpu.VMEM((blocks, 2, tokens, width), F32),
            pltpu.VMEM((blocks, tokens, width), BF16),
            pltpu.VMEM((blocks, tokens, width), BF16),
            pltpu.VMEM((blocks, n_dp, tokens, width), BF16),
            pltpu.VMEM((blocks, 5, width, width), BF16),
            pltpu.VMEM((blocks, width, width), F32),
            dma((4,)),
            dma((n_dp - 1,)), dma((n_dp - 1,)),
            dma((n_dp - 1,)), dma((n_dp - 1,)),
            dma((blocks,)), dma((blocks,)),
            dma((blocks,)), dma((blocks,)),
            dma((blocks, n_dp - 1)), dma((blocks, n_dp - 1)),
        ],
        compiler_params=pltpu.CompilerParams(
            collective_id=0, has_side_effects=True, vmem_limit_bytes=40 * 2**20),
    )(activations, cotangent, base_weight, skew_param))


def solution(mesh):
    return jax.shard_map(
        functools.partial(body, mesh.shape["dp"]),
        mesh=mesh,
        in_specs=(
            P("dp", ("inblk", "outcol")),
            P("dp", "outcol"),
            P("inblk", "outcol"),
            P(("inblk", "outcol"), "dp", None),
        ),
        out_specs=(P("dp", ("inblk", "outcol")), P(("inblk", "outcol"), "dp", None)),
        check_vma=False,
    )
```

```python
import functools

import jax
import jax.numpy as jnp
from jax import lax
from jax.experimental import pallas as pl
from jax.experimental.pallas import tpu as pltpu
from jax.sharding import PartitionSpec as P

F32, BF16 = jnp.float32, jnp.bfloat16
MESH = pl.DeviceIdType.MESH


def mm(left, right):
    return jnp.dot(left, right, preferred_element_type=F32)


def halves(value):
    high = value.astype(BF16)
    return high, (value - high.astype(F32)).astype(BF16)


def mm3(left, right):
    return mm(left[0], right[0]) + (mm(left[0], right[1]) + mm(left[1], right[0]))


def chain(grad, mats, index):
    grad_b = grad.astype(BF16)
    x = mm(mats[index, 0], grad_b) + mm(grad_b, mats[index, 0])
    x_b = x.astype(BF16)
    kx = (x + mm(mats[index, 3], x_b)).astype(BF16)
    lead = 2.0 * grad + x
    dq = (lead + x) + mm(mats[index, 4], x_b)
    dq = dq + mm(lead.astype(BF16), mats[index, 2]) + mm(kx, mats[index, 1])
    return dq - dq.T


def exchange(n_dp, act_hbm, cot_hbm, w_hbm, skew_hbm, ga_ref, gs_ref, mats, act_t, feat,
             skew_own, skew_all, act_all, cot_v, w_v,
             s1_send, s1_recv, part, y_send, y_recv, dq_v,
             loc, skew_s, skew_r, act_s, act_r, s1_s, s1_r, y_s, y_r, f_s, f_r):
    me, out = lax.axis_index("dp"), lax.axis_index("outcol")
    side, core = lax.div(out, 2), lax.rem(out, 2)
    sib = side * 2 + 1 - core
    far = (1 - side) * 2 + core
    far_sib = (1 - side) * 2 + 1 - core
    tokens = cot_v.shape[0]
    blocks, rows, width = skew_own.shape
    peers = [lax.rem(me + step, n_dp) for step in range(1, n_dp)]

    loads = [
        pltpu.make_async_copy(src, dst, loc.at[i])
        for i, (src, dst) in enumerate(
            ((cot_hbm, cot_v), (w_hbm, w_v), (skew_hbm, skew_own), (act_hbm, act_all.at[0]))
        )
    ]
    for load in loads:
        load.start()

    barrier = pltpu.get_barrier_semaphore()
    pl.semaphore_signal(barrier, inc=1, device_id={"outcol": sib}, device_id_type=MESH)
    pl.semaphore_signal(barrier, inc=1, device_id={"outcol": far}, device_id_type=MESH)
    for peer in peers:
        pl.semaphore_signal(barrier, inc=1, device_id={"dp": peer}, device_id_type=MESH)

    def partial_of(owner, block):
        start = pl.multiple_of((owner * blocks + block) * width, width)
        return lax.dot_general(
            cot_v[...], w_v[pl.ds(start, width), :], (((1,), (1,)), ((), ())),
            preferred_element_type=F32,
        )

    def remote(src, dst, send, recv, **where):
        return pltpu.make_async_remote_copy(
            src_ref=src, dst_ref=dst, send_sem=send, recv_sem=recv,
            device_id=where, device_id_type=MESH,
        )

    loads[2].wait()
    skew_all[me] = skew_own[...].astype(skew_all.dtype)
    loads[0].wait()
    loads[1].wait()
    for block in range(blocks):
        s1_send[block, 0] = partial_of(sib, block).astype(BF16)
        s1_send[block, 1] = partial_of(far_sib, block).astype(BF16)

    pl.semaphore_wait(barrier, 1 + n_dp)

    s1 = [remote(s1_send.at[b], s1_recv.at[b], s1_s.at[b], s1_r.at[b], outcol=sib)
          for b in range(blocks)]
    skews = [remote(skew_all.at[me], skew_all.at[me], skew_s.at[i], skew_r.at[i], dp=peer)
             for i, peer in enumerate(peers)]
    acts = [remote(act_hbm, act_all.at[i + 1], act_s.at[i], act_r.at[i], dp=peer)
            for i, peer in enumerate(peers)]
    for copy in s1 + skews + acts:
        copy.start()

    for block in range(blocks):
        part[block, 0] = partial_of(out, block)
        part[block, 1] = partial_of(far, block)

    sides = [remote(y_send.at[b], y_recv.at[b], y_s.at[b], y_r.at[b], outcol=far)
             for b in range(blocks)]
    for block in range(blocks):
        s1[block].wait_recv()
        y_send[block] = (part[block, 1] + s1_recv[block, 1].astype(F32)).astype(BF16)
        sides[block].start()
    loads[3].wait()
    act_t[:, :tokens] = act_all[0].T
    feats = []
    for block in range(blocks):
        sides[block].wait_recv()
        total = part[block, 0] + s1_recv[block, 0].astype(F32) + y_recv[block].astype(F32)
        feat[block, 0] = total.astype(BF16)
        for i, peer in enumerate(peers):
            copy = remote(feat.at[block, 0], feat.at[block, i + 1],
                          f_s.at[block, i], f_r.at[block, i], dp=peer)
            copy.start()
            feats.append(copy)

    for copy in skews:
        copy.wait_recv()
    eye = (lax.broadcasted_iota(jnp.int32, (width, width), 0)
           == lax.broadcasted_iota(jnp.int32, (width, width), 1)).astype(F32)
    for block in range(blocks):
        given = skew_all[:, block].reshape(width, width).astype(F32)
        m1 = given.T - given
        m1_h = halves(m1)
        m2 = mm3(m1_h, m1_h)
        m2_h = halves(m2)
        m4 = mm3(m2_h, m2_h)
        k0 = 2.0 * m1 + m2
        k0_h = halves(k0)
        c2 = mm3(k0_h, m2_h)
        c4 = mm3(k0_h, halves(m4))
        n0 = m2 + m4
        rot_t = (eye + ((k0 + n0) + (c2 + c4))).astype(BF16)
        ga_ref[:, block * width:(block + 1) * width] = mm(feat[block, 0], rot_t).astype(BF16)
        mats[block, 0] = m1_h[0]
        mats[block, 1] = m2_h[0]
        mats[block, 2] = n0.astype(BF16)
        mats[block, 3] = k0_h[0]
        mats[block, 4] = (k0 + m2 + c2).astype(BF16)

    for slot in range(1, n_dp):
        acts[slot - 1].wait_recv()
        act_t[:, slot * tokens:(slot + 1) * tokens] = act_all[slot].T

    for block in range(blocks):
        for copy in feats[block * (n_dp - 1):(block + 1) * (n_dp - 1)]:
            copy.wait_recv()
        if block < blocks - 1:
            grad = mm(act_t[block * width:(block + 1) * width, :],
                      feat[block].reshape(n_dp * tokens, width))
            dq_v[...] = chain(grad, mats, block)
            gs_ref[block] = dq_v[pl.ds(pl.multiple_of(me * rows, rows), rows), :]

    for copy in s1 + skews + acts + sides + feats:
        copy.wait_send()


def finish(n_dp, ga_ref, gs_ref, mats, act_t, feat, ga_out, gs_out, dq_v, sems):
    me = lax.axis_index("dp")
    blocks, rows, width = gs_out.shape
    last = blocks - 1
    writes = [pltpu.make_async_copy(ga_ref, ga_out, sems.at[0])]
    writes += [pltpu.make_async_copy(gs_ref.at[b], gs_out.at[b], sems.at[b + 1])
               for b in range(last)]
    for write in writes:
        write.start()
    grad = mm(act_t[last * width:, :], feat[last].reshape(-1, width))
    dq_v[...] = chain(grad, mats, last)
    end = pltpu.make_async_copy(dq_v.at[pl.ds(pl.multiple_of(me * rows, rows), rows)],
                                gs_out.at[last], sems.at[blocks])
    end.start()
    for write in writes + [end]:
        write.wait()


def body(n_dp, activations, cotangent, base_weight, skew_param):
    tokens, own = activations.shape
    blocks, rows, width = skew_param.shape
    wire = BF16 if rows % 16 == 0 else F32
    dma = pltpu.SemaphoreType.DMA
    vmem = pl.BlockSpec(memory_space=pltpu.VMEM)
    outs = (jax.ShapeDtypeStruct((tokens, own), BF16),
            jax.ShapeDtypeStruct((blocks, rows, width), F32))
    activations, cotangent, base_weight, skew_param = (
        pltpu.with_memory_space_constraint(each, pltpu.HBM)
        for each in (activations, cotangent, base_weight, skew_param))
    parts = pl.pallas_call(
        functools.partial(exchange, n_dp),
        out_shape=(outs[0],
                   jax.ShapeDtypeStruct((blocks - 1, rows, width), F32),
                   jax.ShapeDtypeStruct((blocks, 5, width, width), BF16),
                   jax.ShapeDtypeStruct((own, n_dp * tokens), BF16),
                   jax.ShapeDtypeStruct((blocks, n_dp, tokens, width), BF16)),
        in_specs=[pl.BlockSpec(memory_space=pltpu.HBM)] * 4,
        out_specs=[vmem] * 5,
        scratch_shapes=[
            pltpu.VMEM((blocks, rows, width), F32),
            pltpu.VMEM((n_dp, blocks, rows, width), wire),
            pltpu.VMEM((n_dp, tokens, own), BF16),
            pltpu.VMEM(cotangent.shape, BF16),
            pltpu.VMEM(base_weight.shape, BF16),
            pltpu.VMEM((blocks, 2, tokens, width), BF16),
            pltpu.VMEM((blocks, 2, tokens, width), BF16),
            pltpu.VMEM((blocks, 2, tokens, width), F32),
            pltpu.VMEM((blocks, tokens, width), BF16),
            pltpu.VMEM((blocks, tokens, width), BF16),
            pltpu.VMEM((width, width), F32),
            dma((4,)),
            dma((n_dp - 1,)), dma((n_dp - 1,)),
            dma((n_dp - 1,)), dma((n_dp - 1,)),
            dma((blocks,)), dma((blocks,)),
            dma((blocks,)), dma((blocks,)),
            dma((blocks, n_dp - 1)), dma((blocks, n_dp - 1)),
        ],
        compiler_params=pltpu.CompilerParams(
            collective_id=0, has_side_effects=True, vmem_limit_bytes=32 * 2**20),
    )(activations, cotangent, base_weight, skew_param)
    return tuple(pl.pallas_call(
        functools.partial(finish, n_dp),
        out_shape=outs,
        in_specs=[vmem] * 5,
        out_specs=[pl.BlockSpec(memory_space=pltpu.HBM)] * 2,
        scratch_shapes=[pltpu.VMEM((width, width), F32), dma((blocks + 1,))],
        compiler_params=pltpu.CompilerParams(vmem_limit_bytes=32 * 2**20),
    )(*parts))


def solution(mesh):
    return jax.shard_map(
        functools.partial(body, mesh.shape["dp"]),
        mesh=mesh,
        in_specs=(
            P("dp", ("inblk", "outcol")),
            P("dp", "outcol"),
            P("inblk", "outcol"),
            P(("inblk", "outcol"), "dp", None),
        ),
        out_specs=(P("dp", ("inblk", "outcol")), P(("inblk", "outcol"), "dp", None)),
        check_vma=False,
    )
```

```python
import functools

import jax
import jax.numpy as jnp
from jax import lax
from jax.experimental import pallas as pl
from jax.experimental.pallas import tpu as pltpu
from jax.sharding import PartitionSpec as P

F32, BF16 = jnp.float32, jnp.bfloat16
MESH = pl.DeviceIdType.MESH


def mm(left, right):
    return jnp.dot(left, right, preferred_element_type=F32)


def halves(value):
    high = value.astype(BF16)
    return high, (value - high.astype(F32)).astype(BF16)


def mm3(left, right):
    return mm(left[0], right[0]) + (mm(left[0], right[1]) + mm(left[1], right[0]))


def chain(grad, mats, index):
    grad_b = grad.astype(BF16)
    x = mm(mats[index, 0], grad_b) + mm(grad_b, mats[index, 0])
    x_b = x.astype(BF16)
    kx = (x + mm(mats[index, 3], x_b)).astype(BF16)
    lead = 2.0 * grad + x
    dq = (lead + x) + mm(mats[index, 4], x_b)
    dq = dq + mm(lead.astype(BF16), mats[index, 2]) + mm(kx, mats[index, 1])
    return dq - dq.T


def exchange(n_dp, act_hbm, cot_hbm, w_hbm, skew_hbm, ga_ref, gs_ref, mats, act_t, feat,
             skew_own, skew_all, act_all, cot_v, w_v,
             s1_send, s1_recv, part, y_send, y_recv, rot_t, dq_v,
             loc, skew_s, skew_r, act_s, act_r, s1_s, s1_r, y_s, y_r, f_s, f_r):
    me, out = lax.axis_index("dp"), lax.axis_index("outcol")
    side, core = lax.div(out, 2), lax.rem(out, 2)
    sib = side * 2 + 1 - core
    far = (1 - side) * 2 + core
    far_sib = (1 - side) * 2 + 1 - core
    tokens = cot_v.shape[0]
    blocks, rows, width = skew_own.shape
    peers = [lax.rem(me + step, n_dp) for step in range(1, n_dp)]

    loads = [
        pltpu.make_async_copy(src, dst, loc.at[i])
        for i, (src, dst) in enumerate(
            ((cot_hbm, cot_v), (w_hbm, w_v), (skew_hbm, skew_own), (act_hbm, act_all.at[0]))
        )
    ]
    for load in loads:
        load.start()

    barrier = pltpu.get_barrier_semaphore()
    pl.semaphore_signal(barrier, inc=1, device_id={"outcol": sib}, device_id_type=MESH)
    pl.semaphore_signal(barrier, inc=1, device_id={"outcol": far}, device_id_type=MESH)
    for peer in peers:
        pl.semaphore_signal(barrier, inc=1, device_id={"dp": peer}, device_id_type=MESH)

    def partial_of(owner, block):
        start = pl.multiple_of((owner * blocks + block) * width, width)
        return lax.dot_general(
            cot_v[...], w_v[pl.ds(start, width), :], (((1,), (1,)), ((), ())),
            preferred_element_type=F32,
        )

    def remote(src, dst, send, recv, **where):
        return pltpu.make_async_remote_copy(
            src_ref=src, dst_ref=dst, send_sem=send, recv_sem=recv,
            device_id=where, device_id_type=MESH,
        )

    loads[2].wait()
    skew_all[me] = skew_own[...].astype(skew_all.dtype)
    loads[0].wait()
    loads[1].wait()
    for block in range(blocks):
        s1_send[block, 0] = partial_of(sib, block).astype(BF16)
        s1_send[block, 1] = partial_of(far_sib, block).astype(BF16)

    pl.semaphore_wait(barrier, 1 + n_dp)

    s1 = [remote(s1_send.at[b], s1_recv.at[b], s1_s.at[b], s1_r.at[b], outcol=sib)
          for b in range(blocks)]
    skews = [remote(skew_all.at[me], skew_all.at[me], skew_s.at[i], skew_r.at[i], dp=peer)
             for i, peer in enumerate(peers)]
    acts = [remote(act_hbm, act_all.at[i + 1], act_s.at[i], act_r.at[i], dp=peer)
            for i, peer in enumerate(peers)]
    for copy in s1 + skews + acts:
        copy.start()

    for block in range(blocks):
        part[block, 0] = partial_of(out, block)
        part[block, 1] = partial_of(far, block)

    sides = [remote(y_send.at[b], y_recv.at[b], y_s.at[b], y_r.at[b], outcol=far)
             for b in range(blocks)]
    for block in range(blocks):
        s1[block].wait_recv()
        y_send[block] = (part[block, 1] + s1_recv[block, 1].astype(F32)).astype(BF16)
        sides[block].start()
    loads[3].wait()
    act_t[:, :tokens] = act_all[0].T
    for copy in skews:
        copy.wait_recv()
    eye = (lax.broadcasted_iota(jnp.int32, (width, width), 0)
           == lax.broadcasted_iota(jnp.int32, (width, width), 1)).astype(F32)
    feats = []
    for block in range(blocks):
        given = skew_all[:, block].reshape(width, width).astype(F32)
        m1 = given.T - given
        m1_h = halves(m1)
        m2 = mm3(m1_h, m1_h)
        m2_h = halves(m2)
        m4 = mm3(m2_h, m2_h)
        k0 = 2.0 * m1 + m2
        k0_h = halves(k0)
        c2 = mm3(k0_h, m2_h)
        c4 = mm3(k0_h, halves(m4))
        n0 = m2 + m4
        rot_t[block] = (eye + ((k0 + n0) + (c2 + c4))).astype(BF16)
        mats[block, 0] = m1_h[0]
        mats[block, 1] = m2_h[0]
        mats[block, 2] = n0.astype(BF16)
        mats[block, 3] = k0_h[0]
        mats[block, 4] = (k0 + m2 + c2).astype(BF16)

        sides[block].wait_recv()
        total = part[block, 0] + s1_recv[block, 0].astype(F32) + y_recv[block].astype(F32)
        feat[block, 0] = total.astype(BF16)
        for i, peer in enumerate(peers):
            copy = remote(feat.at[block, 0], feat.at[block, i + 1],
                          f_s.at[block, i], f_r.at[block, i], dp=peer)
            copy.start()
            feats.append(copy)
    for block in range(blocks):
        ga_ref[:, block * width:(block + 1) * width] = mm(
            feat[block, 0], rot_t[block]).astype(BF16)

    for slot in range(1, n_dp):
        acts[slot - 1].wait_recv()
        act_t[:, slot * tokens:(slot + 1) * tokens] = act_all[slot].T

    for block in range(blocks):
        for copy in feats[block * (n_dp - 1):(block + 1) * (n_dp - 1)]:
            copy.wait_recv()
        if block < blocks - 1:
            grad = mm(act_t[block * width:(block + 1) * width, :],
                      feat[block].reshape(n_dp * tokens, width))
            dq_v[...] = chain(grad, mats, block)
            gs_ref[block] = dq_v[pl.ds(pl.multiple_of(me * rows, rows), rows), :]

    for copy in s1 + skews + acts + sides + feats:
        copy.wait_send()


def finish(n_dp, ga_ref, gs_ref, mats, act_t, feat, ga_out, gs_out, dq_v, sems):
    me = lax.axis_index("dp")
    blocks, rows, width = gs_out.shape
    last = blocks - 1
    writes = [pltpu.make_async_copy(ga_ref, ga_out, sems.at[0])]
    writes += [pltpu.make_async_copy(gs_ref.at[b], gs_out.at[b], sems.at[b + 1])
               for b in range(last)]
    for write in writes:
        write.start()
    grad = mm(act_t[last * width:, :], feat[last].reshape(-1, width))
    dq_v[...] = chain(grad, mats, last)
    end = pltpu.make_async_copy(dq_v.at[pl.ds(pl.multiple_of(me * rows, rows), rows)],
                                gs_out.at[last], sems.at[blocks])
    end.start()
    for write in writes + [end]:
        write.wait()


def body(n_dp, activations, cotangent, base_weight, skew_param):
    tokens, own = activations.shape
    blocks, rows, width = skew_param.shape
    wire = BF16 if rows % 16 == 0 else F32
    dma = pltpu.SemaphoreType.DMA
    vmem = pl.BlockSpec(memory_space=pltpu.VMEM)
    outs = (jax.ShapeDtypeStruct((tokens, own), BF16),
            jax.ShapeDtypeStruct((blocks, rows, width), F32))
    activations, cotangent, base_weight, skew_param = (
        pltpu.with_memory_space_constraint(each, pltpu.HBM)
        for each in (activations, cotangent, base_weight, skew_param))
    parts = pl.pallas_call(
        functools.partial(exchange, n_dp),
        out_shape=(outs[0],
                   jax.ShapeDtypeStruct((blocks - 1, rows, width), F32),
                   jax.ShapeDtypeStruct((blocks, 5, width, width), BF16),
                   jax.ShapeDtypeStruct((own, n_dp * tokens), BF16),
                   jax.ShapeDtypeStruct((blocks, n_dp, tokens, width), BF16)),
        in_specs=[pl.BlockSpec(memory_space=pltpu.HBM)] * 4,
        out_specs=[vmem] * 5,
        scratch_shapes=[
            pltpu.VMEM((blocks, rows, width), F32),
            pltpu.VMEM((n_dp, blocks, rows, width), wire),
            pltpu.VMEM((n_dp, tokens, own), BF16),
            pltpu.VMEM(cotangent.shape, BF16),
            pltpu.VMEM(base_weight.shape, BF16),
            pltpu.VMEM((blocks, 2, tokens, width), BF16),
            pltpu.VMEM((blocks, 2, tokens, width), BF16),
            pltpu.VMEM((blocks, 2, tokens, width), F32),
            pltpu.VMEM((blocks, tokens, width), BF16),
            pltpu.VMEM((blocks, tokens, width), BF16),
            pltpu.VMEM((blocks, width, width), BF16),
            pltpu.VMEM((width, width), F32),
            dma((4,)),
            dma((n_dp - 1,)), dma((n_dp - 1,)),
            dma((n_dp - 1,)), dma((n_dp - 1,)),
            dma((blocks,)), dma((blocks,)),
            dma((blocks,)), dma((blocks,)),
            dma((blocks, n_dp - 1)), dma((blocks, n_dp - 1)),
        ],
        compiler_params=pltpu.CompilerParams(
            collective_id=0, has_side_effects=True, vmem_limit_bytes=32 * 2**20),
    )(activations, cotangent, base_weight, skew_param)
    return tuple(pl.pallas_call(
        functools.partial(finish, n_dp),
        out_shape=outs,
        in_specs=[vmem] * 5,
        out_specs=[pl.BlockSpec(memory_space=pltpu.HBM)] * 2,
        scratch_shapes=[pltpu.VMEM((width, width), F32), dma((blocks + 1,))],
        compiler_params=pltpu.CompilerParams(vmem_limit_bytes=32 * 2**20),
    )(*parts))


def solution(mesh):
    return jax.shard_map(
        functools.partial(body, mesh.shape["dp"]),
        mesh=mesh,
        in_specs=(
            P("dp", ("inblk", "outcol")),
            P("dp", "outcol"),
            P("inblk", "outcol"),
            P(("inblk", "outcol"), "dp", None),
        ),
        out_specs=(P("dp", ("inblk", "outcol")), P(("inblk", "outcol"), "dp", None)),
        check_vma=False,
    )
```

```python
import functools

import jax
import jax.numpy as jnp
from jax import lax
from jax.experimental import pallas as pl
from jax.experimental.pallas import tpu as pltpu
from jax.sharding import PartitionSpec as P

F32, BF16 = jnp.float32, jnp.bfloat16
MESH = pl.DeviceIdType.MESH


def mm(left, right):
    return jnp.dot(left, right, preferred_element_type=F32)


def halves(value):
    high = value.astype(BF16)
    return high, (value - high.astype(F32)).astype(BF16)


def mm3(left, right):
    return mm(left[0], right[0]) + (mm(left[0], right[1]) + mm(left[1], right[0]))


def grad_of(n_dp, feat, act_all, block):
    width = feat.shape[2]
    columns = slice(block * width, (block + 1) * width)
    grad = mm(feat[block, 0], act_all[0, :, columns])
    for slot in range(1, n_dp):
        grad = grad + mm(feat[block, slot], act_all[slot, :, columns])
    return grad


def chain(grad, mats, index):
    grad_b = grad.astype(BF16)
    x = mm(mats[index, 0], grad_b) + mm(grad_b, mats[index, 0])
    x_b = x.astype(BF16)
    kx = (x + mm(mats[index, 3], x_b)).astype(BF16)
    lead = 2.0 * grad + x
    dq = (lead + x) + mm(mats[index, 4], x_b)
    dq = dq + mm(lead.astype(BF16), mats[index, 2]) + mm(kx, mats[index, 1])
    return dq.T - dq


def exchange(n_dp, act_hbm, cot_hbm, w_hbm, skew_hbm, ga_ref, gs_ref, mats, act_all, feat,
             skew_own, skew_all, cot_v, cot_t, w_v,
             s1_send, s1_recv, part, y_send, y_recv, rot, dq_v,
             loc, skew_s, skew_r, act_s, act_r, s1_s, s1_r, y_s, y_r, f_s, f_r):
    me, out = lax.axis_index("dp"), lax.axis_index("outcol")
    side, core = lax.div(out, 2), lax.rem(out, 2)
    sib = side * 2 + 1 - core
    far = (1 - side) * 2 + core
    far_sib = (1 - side) * 2 + 1 - core
    blocks, rows, width = skew_own.shape
    peers = [lax.rem(me + step, n_dp) for step in range(1, n_dp)]

    loads = [
        pltpu.make_async_copy(src, dst, loc.at[i])
        for i, (src, dst) in enumerate(
            ((skew_hbm, skew_own), (cot_hbm, cot_v), (w_hbm, w_v), (act_hbm, act_all.at[0]))
        )
    ]
    for load in loads:
        load.start()

    barrier = pltpu.get_barrier_semaphore()
    pl.semaphore_signal(barrier, inc=1, device_id={"outcol": sib}, device_id_type=MESH)
    pl.semaphore_signal(barrier, inc=1, device_id={"outcol": far}, device_id_type=MESH)
    for peer in peers:
        pl.semaphore_signal(barrier, inc=1, device_id={"dp": peer}, device_id_type=MESH)

    def partial_of(owner, block):
        start = pl.multiple_of((owner * blocks + block) * width, width)
        return mm(w_v[pl.ds(start, width), :], cot_t[...])

    def remote(src, dst, send, recv, **where):
        return pltpu.make_async_remote_copy(
            src_ref=src, dst_ref=dst, send_sem=send, recv_sem=recv,
            device_id=where, device_id_type=MESH,
        )

    s1 = [remote(s1_send.at[b], s1_recv.at[b], s1_s.at[b], s1_r.at[b], outcol=sib)
          for b in range(blocks)]
    skews = [remote(skew_all.at[me], skew_all.at[me], skew_s.at[i], skew_r.at[i], dp=peer)
             for i, peer in enumerate(peers)]
    acts = [remote(act_hbm, act_all.at[i + 1], act_s.at[i], act_r.at[i], dp=peer)
            for i, peer in enumerate(peers)]

    loads[0].wait()
    skew_all[me] = skew_own[...].astype(skew_all.dtype)
    loads[1].wait()
    cot_t[...] = cot_v[...].T
    pl.semaphore_wait(barrier, 1 + n_dp)
    for copy in skews:
        copy.start()

    loads[2].wait()
    for block in range(blocks):
        s1_send[block, 0] = partial_of(sib, block).astype(BF16)
        s1_send[block, 1] = partial_of(far_sib, block).astype(BF16)
        s1[block].start()
    for block in range(blocks):
        part[block, 1] = partial_of(far, block)
        part[block, 0] = partial_of(out, block)

    sides = [remote(y_send.at[b], y_recv.at[b], y_s.at[b], y_r.at[b], outcol=far)
             for b in range(blocks)]
    for block in range(blocks):
        s1[block].wait_recv()
        y_send[block] = (part[block, 1] + s1_recv[block, 1].astype(F32)).astype(BF16)
        sides[block].start()
    for copy in acts:
        copy.start()
    for copy in skews:
        copy.wait_recv()
    eye = (lax.broadcasted_iota(jnp.int32, (width, width), 0)
           == lax.broadcasted_iota(jnp.int32, (width, width), 1)).astype(F32)
    feats = []
    for block in range(blocks):
        given = skew_all[:, block].reshape(width, width).astype(F32)
        m1 = given - given.T
        m1_h = halves(m1)
        m2 = mm3(m1_h, m1_h)
        m2_h = halves(m2)
        m4 = mm3(m2_h, m2_h)
        k0 = 2.0 * m1 + m2
        k0_h = halves(k0)
        n0 = m2 + m4
        n0_h = halves(n0)
        rot[block] = (eye + ((k0 + n0) + mm3(k0_h, n0_h))).astype(BF16)
        mats[block, 0] = m1_h[0]
        mats[block, 1] = m2_h[0]
        mats[block, 2] = n0_h[0]
        mats[block, 3] = k0_h[0]
        mats[block, 4] = (k0 + m2 + mm(k0_h[0], m2_h[0])).astype(BF16)

        sides[block].wait_recv()
        total = part[block, 0] + s1_recv[block, 0].astype(F32) + y_recv[block].astype(F32)
        feat[block, 0] = total.astype(BF16)
        for i, peer in enumerate(peers):
            copy = remote(feat.at[block, 0], feat.at[block, i + 1],
                          f_s.at[block, i], f_r.at[block, i], dp=peer)
            copy.start()
            feats.append(copy)
    for block in range(blocks):
        ga_ref[:, block * width:(block + 1) * width] = mm(
            rot[block], feat[block, 0]).T.astype(BF16)

    loads[3].wait()
    for copy in acts:
        copy.wait_recv()

    for block in range(blocks):
        for copy in feats[block * (n_dp - 1):(block + 1) * (n_dp - 1)]:
            copy.wait_recv()
        if block < blocks - 1:
            dq_v[...] = chain(grad_of(n_dp, feat, act_all, block), mats, block)
            gs_ref[block] = dq_v[pl.ds(pl.multiple_of(me * rows, rows), rows), :]

    for copy in s1 + skews + acts + sides + feats:
        copy.wait_send()


def finish(n_dp, ga_ref, gs_ref, mats, act_all, feat, ga_out, gs_out, dq_v, sems):
    me = lax.axis_index("dp")
    blocks, rows, width = gs_out.shape
    last = blocks - 1
    writes = [pltpu.make_async_copy(ga_ref, ga_out, sems.at[0])]
    writes += [pltpu.make_async_copy(gs_ref.at[b], gs_out.at[b], sems.at[b + 1])
               for b in range(last)]
    for write in writes:
        write.start()
    dq_v[...] = chain(grad_of(n_dp, feat, act_all, last), mats, last)
    end = pltpu.make_async_copy(dq_v.at[pl.ds(pl.multiple_of(me * rows, rows), rows)],
                                gs_out.at[last], sems.at[blocks])
    end.start()
    for write in writes + [end]:
        write.wait()


def body(n_dp, activations, cotangent, base_weight, skew_param):
    tokens, own = activations.shape
    blocks, rows, width = skew_param.shape
    wire = BF16 if rows % 16 == 0 else F32
    dma = pltpu.SemaphoreType.DMA
    vmem = pl.BlockSpec(memory_space=pltpu.VMEM)
    outs = (jax.ShapeDtypeStruct((tokens, own), BF16),
            jax.ShapeDtypeStruct((blocks, rows, width), F32))
    activations, cotangent, base_weight, skew_param = (
        pltpu.with_memory_space_constraint(each, pltpu.HBM)
        for each in (activations, cotangent, base_weight, skew_param))
    parts = pl.pallas_call(
        functools.partial(exchange, n_dp),
        out_shape=(outs[0],
                   jax.ShapeDtypeStruct((blocks - 1, rows, width), F32),
                   jax.ShapeDtypeStruct((blocks, 5, width, width), BF16),
                   jax.ShapeDtypeStruct((n_dp, tokens, own), BF16),
                   jax.ShapeDtypeStruct((blocks, n_dp, width, tokens), BF16)),
        in_specs=[pl.BlockSpec(memory_space=pltpu.HBM)] * 4,
        out_specs=[vmem] * 5,
        scratch_shapes=[
            pltpu.VMEM((blocks, rows, width), F32),
            pltpu.VMEM((n_dp, blocks, rows, width), wire),
            pltpu.VMEM(cotangent.shape, BF16),
            pltpu.VMEM(cotangent.shape[::-1], BF16),
            pltpu.VMEM(base_weight.shape, BF16),
            pltpu.VMEM((blocks, 2, width, tokens), BF16),
            pltpu.VMEM((blocks, 2, width, tokens), BF16),
            pltpu.VMEM((blocks, 2, width, tokens), F32),
            pltpu.VMEM((blocks, width, tokens), BF16),
            pltpu.VMEM((blocks, width, tokens), BF16),
            pltpu.VMEM((blocks, width, width), BF16),
            pltpu.VMEM((width, width), F32),
            dma((4,)),
            dma((n_dp - 1,)), dma((n_dp - 1,)),
            dma((n_dp - 1,)), dma((n_dp - 1,)),
            dma((blocks,)), dma((blocks,)),
            dma((blocks,)), dma((blocks,)),
            dma((blocks, n_dp - 1)), dma((blocks, n_dp - 1)),
        ],
        compiler_params=pltpu.CompilerParams(
            collective_id=0, has_side_effects=True, vmem_limit_bytes=32 * 2**20),
    )(activations, cotangent, base_weight, skew_param)
    return tuple(pl.pallas_call(
        functools.partial(finish, n_dp),
        out_shape=outs,
        in_specs=[vmem] * 5,
        out_specs=[pl.BlockSpec(memory_space=pltpu.HBM)] * 2,
        scratch_shapes=[pltpu.VMEM((width, width), F32), dma((blocks + 1,))],
        compiler_params=pltpu.CompilerParams(vmem_limit_bytes=32 * 2**20),
    )(*parts))


def solution(mesh):
    return jax.shard_map(
        functools.partial(body, mesh.shape["dp"]),
        mesh=mesh,
        in_specs=(
            P("dp", ("inblk", "outcol")),
            P("dp", "outcol"),
            P("inblk", "outcol"),
            P(("inblk", "outcol"), "dp", None),
        ),
        out_specs=(P("dp", ("inblk", "outcol")), P(("inblk", "outcol"), "dp", None)),
        check_vma=False,
    )
```

```python
import functools

import jax
import jax.numpy as jnp
from jax import lax
from jax.experimental import pallas as pl
from jax.experimental.pallas import tpu as pltpu
from jax.sharding import PartitionSpec as P

F32, BF16 = jnp.float32, jnp.bfloat16
MESH = pl.DeviceIdType.MESH


def mm(left, right):
    return jnp.dot(left, right, preferred_element_type=F32)


def halves(value):
    high = value.astype(BF16)
    return high, (value - high.astype(F32)).astype(BF16)


def mm3(left, right):
    return mm(left[0], right[0]) + (mm(left[0], right[1]) + mm(left[1], right[0]))


def grad_of(n_dp, feat, act_all, block):
    width = feat.shape[2]
    columns = slice(block * width, (block + 1) * width)
    grad = mm(feat[block, 0], act_all[0, :, columns])
    for slot in range(1, n_dp):
        grad = grad + mm(feat[block, slot], act_all[slot, :, columns])
    return grad


def chain(grad, mats):
    grad_b = grad.astype(BF16)
    x = mm(mats[0], grad_b) + mm(grad_b, mats[0])
    x_b = x.astype(BF16)
    kx = (x + mm(mats[3], x_b)).astype(BF16)
    lead = 2.0 * grad + x
    dq = (lead + x) + mm(mats[4], x_b)
    dq = dq + mm(lead.astype(BF16), mats[2]) + mm(kx, mats[1])
    return dq.T - dq


def pair_exchange(act_hbm, cot_hbm, w_hbm, skew_hbm, ga_ref, gs_ref,
                  skew_own, skew_all, act_pair, cot_v, cot_t, w_v,
                  s1_send, s1_recv, part, y_send, y_recv, feat, feat_in, rot, dq_v,
                  gs_send, gs_recv,
                  loc, x_s, x_r, s1_s, s1_r, y_s, y_r):
    me, out = lax.axis_index("dp"), lax.axis_index("outcol")
    other = 1 - me
    side, core = lax.div(out, 2), lax.rem(out, 2)
    sib = side * 2 + 1 - core
    far = (1 - side) * 2 + core
    far_sib = (1 - side) * 2 + 1 - core
    blocks, rows, width = skew_own.shape
    order = (other, me)

    def columns(block):
        return pl.ds(pl.multiple_of(block * width, width), width)

    def rows_of(device):
        return pl.ds(pl.multiple_of(device * rows, rows), rows)

    loads = [
        pltpu.make_async_copy(src, dst, loc.at[i])
        for i, (src, dst) in enumerate((
            (skew_hbm, skew_own), (cot_hbm, cot_v), (w_hbm, w_v),
            (act_hbm.at[:, columns(me)], act_pair.at[0])))
    ]
    for load in loads:
        load.start()

    barrier = pltpu.get_barrier_semaphore()
    pl.semaphore_signal(barrier, inc=1, device_id={"outcol": sib}, device_id_type=MESH)
    pl.semaphore_signal(barrier, inc=1, device_id={"outcol": far}, device_id_type=MESH)
    pl.semaphore_signal(barrier, inc=1, device_id={"dp": other}, device_id_type=MESH)

    def partial_of(owner, block):
        start = pl.multiple_of((owner * blocks + block) * width, width)
        return mm(w_v[pl.ds(start, width), :], cot_t[...])

    def remote(src, dst, send, recv, **where):
        return pltpu.make_async_remote_copy(
            src_ref=src, dst_ref=dst, send_sem=send, recv_sem=recv,
            device_id=where, device_id_type=MESH,
        )

    s1 = [remote(s1_send.at[k], s1_recv.at[k], s1_s.at[k], s1_r.at[k], outcol=sib)
          for k in range(2)]
    sides = [remote(y_send.at[k], y_recv.at[k], y_s.at[k], y_r.at[k], outcol=far)
             for k in range(2)]
    skews = remote(skew_all.at[me], skew_all.at[me], x_s.at[0], x_r.at[0], dp=other)
    acts = remote(act_hbm.at[:, columns(other)], act_pair.at[1], x_s.at[1], x_r.at[1], dp=other)
    feats = remote(feat.at[0], feat_in, x_s.at[2], x_r.at[2], dp=other)
    back = remote(gs_send, gs_recv, x_s.at[3], x_r.at[3], dp=other)

    loads[0].wait()
    skew_all[me] = skew_own[...].astype(skew_all.dtype)
    loads[1].wait()
    cot_t[...] = cot_v[...].T
    pl.semaphore_wait(barrier, 3)
    skews.start()

    loads[2].wait()
    for k, block in enumerate(order):
        s1_send[k, 0] = partial_of(sib, block).astype(BF16)
        s1_send[k, 1] = partial_of(far_sib, block).astype(BF16)
        s1[k].start()
    acts.start()
    for k, block in enumerate(order):
        part[k, 1] = partial_of(far, block)
        part[k, 0] = partial_of(out, block)
    for k in range(2):
        s1[k].wait_recv()
        y_send[k] = (part[k, 1] + s1_recv[k, 1].astype(F32)).astype(BF16)
        sides[k].start()

    def features(k):
        sides[k].wait_recv()
        total = part[k, 0] + s1_recv[k, 0].astype(F32) + y_recv[k].astype(F32)
        feat[k] = total.astype(BF16)

    eye = (lax.broadcasted_iota(jnp.int32, (width, width), 0)
           == lax.broadcasted_iota(jnp.int32, (width, width), 1)).astype(F32)

    def series(k, block):
        given = skew_all[:, block].reshape(width, width).astype(F32)
        m1 = given - given.T
        m1_h = halves(m1)
        m2 = mm3(m1_h, m1_h)
        m2_h = halves(m2)
        m4 = mm3(m2_h, m2_h)
        k0 = 2.0 * m1 + m2
        k0_h = halves(k0)
        n0 = m2 + m4
        n0_h = halves(n0)
        rot[k] = (eye + ((k0 + n0) + mm3(k0_h, n0_h))).astype(BF16)
        return m1_h[0], m2_h[0], n0_h[0], k0_h[0], (k0 + m2 + mm(k0_h[0], m2_h[0])).astype(BF16)

    features(0)
    feats.start()
    skews.wait_recv()
    mats = series(1, me)
    features(1)
    loads[3].wait()
    grad = mm(feat[1], act_pair[0])
    acts.wait_recv()
    feats.wait_recv()
    grad = grad + mm(feat_in[...], act_pair[1])
    dq_v[...] = chain(grad, mats)
    gs_send[...] = dq_v[rows_of(other), :].astype(BF16)
    back.start()

    gs_ref[me] = dq_v[rows_of(me), :]
    series(0, other)
    for block, k in ((0, 1 - me), (1, me)):
        ga_ref[:, block * width:(block + 1) * width] = mm(rot[k], feat[k]).T.astype(BF16)
    back.wait_recv()
    gs_ref[other] = gs_recv[...].astype(F32)
    for copy in s1 + sides + [skews, acts, feats, back]:
        copy.wait_send()


def pair_finish(ga_ref, gs_ref, ga_out, gs_out, sems):
    writes = [pltpu.make_async_copy(ga_ref, ga_out, sems.at[0]),
              pltpu.make_async_copy(gs_ref, gs_out, sems.at[1])]
    for write in writes:
        write.start()
    for write in writes:
        write.wait()


def exchange(n_dp, act_hbm, cot_hbm, w_hbm, skew_hbm, ga_ref, gs_ref, mats, act_all, feat,
             skew_own, skew_all, cot_v, cot_t, w_v,
             s1_send, s1_recv, part, y_send, y_recv, rot, dq_v,
             loc, skew_s, skew_r, act_s, act_r, s1_s, s1_r, y_s, y_r, f_s, f_r):
    me, out = lax.axis_index("dp"), lax.axis_index("outcol")
    side, core = lax.div(out, 2), lax.rem(out, 2)
    sib = side * 2 + 1 - core
    far = (1 - side) * 2 + core
    far_sib = (1 - side) * 2 + 1 - core
    blocks, rows, width = skew_own.shape
    peers = [lax.rem(me + step, n_dp) for step in range(1, n_dp)]

    loads = [
        pltpu.make_async_copy(src, dst, loc.at[i])
        for i, (src, dst) in enumerate(
            ((skew_hbm, skew_own), (cot_hbm, cot_v), (w_hbm, w_v), (act_hbm, act_all.at[0]))
        )
    ]
    for load in loads:
        load.start()

    barrier = pltpu.get_barrier_semaphore()
    pl.semaphore_signal(barrier, inc=1, device_id={"outcol": sib}, device_id_type=MESH)
    pl.semaphore_signal(barrier, inc=1, device_id={"outcol": far}, device_id_type=MESH)
    for peer in peers:
        pl.semaphore_signal(barrier, inc=1, device_id={"dp": peer}, device_id_type=MESH)

    def partial_of(owner, block):
        start = pl.multiple_of((owner * blocks + block) * width, width)
        return mm(w_v[pl.ds(start, width), :], cot_t[...])

    def remote(src, dst, send, recv, **where):
        return pltpu.make_async_remote_copy(
            src_ref=src, dst_ref=dst, send_sem=send, recv_sem=recv,
            device_id=where, device_id_type=MESH,
        )

    s1 = [remote(s1_send.at[b], s1_recv.at[b], s1_s.at[b], s1_r.at[b], outcol=sib)
          for b in range(blocks)]
    skews = [remote(skew_all.at[me], skew_all.at[me], skew_s.at[i], skew_r.at[i], dp=peer)
             for i, peer in enumerate(peers)]
    acts = [remote(act_hbm, act_all.at[i + 1], act_s.at[i], act_r.at[i], dp=peer)
            for i, peer in enumerate(peers)]

    loads[0].wait()
    skew_all[me] = skew_own[...].astype(skew_all.dtype)
    loads[1].wait()
    cot_t[...] = cot_v[...].T
    pl.semaphore_wait(barrier, 1 + n_dp)
    for copy in skews:
        copy.start()

    loads[2].wait()
    for block in range(blocks):
        s1_send[block, 0] = partial_of(sib, block).astype(BF16)
        s1_send[block, 1] = partial_of(far_sib, block).astype(BF16)
        s1[block].start()
    for block in range(blocks):
        part[block, 1] = partial_of(far, block)
        part[block, 0] = partial_of(out, block)

    sides = [remote(y_send.at[b], y_recv.at[b], y_s.at[b], y_r.at[b], outcol=far)
             for b in range(blocks)]
    for block in range(blocks):
        s1[block].wait_recv()
        y_send[block] = (part[block, 1] + s1_recv[block, 1].astype(F32)).astype(BF16)
        sides[block].start()
    for copy in acts:
        copy.start()
    for copy in skews:
        copy.wait_recv()
    eye = (lax.broadcasted_iota(jnp.int32, (width, width), 0)
           == lax.broadcasted_iota(jnp.int32, (width, width), 1)).astype(F32)
    feats = []
    for block in range(blocks):
        given = skew_all[:, block].reshape(width, width).astype(F32)
        m1 = given - given.T
        m1_h = halves(m1)
        m2 = mm3(m1_h, m1_h)
        m2_h = halves(m2)
        m4 = mm3(m2_h, m2_h)
        k0 = 2.0 * m1 + m2
        k0_h = halves(k0)
        n0 = m2 + m4
        n0_h = halves(n0)
        rot[block] = (eye + ((k0 + n0) + mm3(k0_h, n0_h))).astype(BF16)
        mats[block, 0] = m1_h[0]
        mats[block, 1] = m2_h[0]
        mats[block, 2] = n0_h[0]
        mats[block, 3] = k0_h[0]
        mats[block, 4] = (k0 + m2 + mm(k0_h[0], m2_h[0])).astype(BF16)

        sides[block].wait_recv()
        total = part[block, 0] + s1_recv[block, 0].astype(F32) + y_recv[block].astype(F32)
        feat[block, 0] = total.astype(BF16)
        for i, peer in enumerate(peers):
            copy = remote(feat.at[block, 0], feat.at[block, i + 1],
                          f_s.at[block, i], f_r.at[block, i], dp=peer)
            copy.start()
            feats.append(copy)
    for block in range(blocks):
        ga_ref[:, block * width:(block + 1) * width] = mm(
            rot[block], feat[block, 0]).T.astype(BF16)

    loads[3].wait()
    for copy in acts:
        copy.wait_recv()

    for block in range(blocks):
        for copy in feats[block * (n_dp - 1):(block + 1) * (n_dp - 1)]:
            copy.wait_recv()
        if block < blocks - 1:
            dq_v[...] = chain(grad_of(n_dp, feat, act_all, block), mats.at[block])
            gs_ref[block] = dq_v[pl.ds(pl.multiple_of(me * rows, rows), rows), :]

    for copy in s1 + skews + acts + sides + feats:
        copy.wait_send()


def finish(n_dp, ga_ref, gs_ref, mats, act_all, feat, ga_out, gs_out, dq_v, sems):
    me = lax.axis_index("dp")
    blocks, rows, width = gs_out.shape
    last = blocks - 1
    writes = [pltpu.make_async_copy(ga_ref, ga_out, sems.at[0])]
    writes += [pltpu.make_async_copy(gs_ref.at[b], gs_out.at[b], sems.at[b + 1])
               for b in range(last)]
    for write in writes:
        write.start()
    dq_v[...] = chain(grad_of(n_dp, feat, act_all, last), mats.at[last])
    end = pltpu.make_async_copy(dq_v.at[pl.ds(pl.multiple_of(me * rows, rows), rows)],
                                gs_out.at[last], sems.at[blocks])
    end.start()
    for write in writes + [end]:
        write.wait()


def body(n_dp, activations, cotangent, base_weight, skew_param):
    tokens, own = activations.shape
    blocks, rows, width = skew_param.shape
    wire = BF16 if rows % 16 == 0 else F32
    dma = pltpu.SemaphoreType.DMA
    vmem = pl.BlockSpec(memory_space=pltpu.VMEM)
    outs = (jax.ShapeDtypeStruct((tokens, own), BF16),
            jax.ShapeDtypeStruct((blocks, rows, width), F32))
    activations, cotangent, base_weight, skew_param = (
        pltpu.with_memory_space_constraint(each, pltpu.HBM)
        for each in (activations, cotangent, base_weight, skew_param))
    if n_dp == 2 and blocks == 2 and wire == BF16:
        pairs = pl.pallas_call(
            pair_exchange,
            out_shape=outs,
            in_specs=[pl.BlockSpec(memory_space=pltpu.HBM)] * 4,
            out_specs=[vmem] * 2,
            scratch_shapes=[
                pltpu.VMEM((2, rows, width), F32),
                pltpu.VMEM((2, 2, rows, width), BF16),
                pltpu.VMEM((2, tokens, width), BF16),
                pltpu.VMEM(cotangent.shape, BF16),
                pltpu.VMEM(cotangent.shape[::-1], BF16),
                pltpu.VMEM(base_weight.shape, BF16),
                pltpu.VMEM((2, 2, width, tokens), BF16),
                pltpu.VMEM((2, 2, width, tokens), BF16),
                pltpu.VMEM((2, 2, width, tokens), F32),
                pltpu.VMEM((2, width, tokens), BF16),
                pltpu.VMEM((2, width, tokens), BF16),
                pltpu.VMEM((2, width, tokens), BF16),
                pltpu.VMEM((width, tokens), BF16),
                pltpu.VMEM((2, width, width), BF16),
                pltpu.VMEM((width, width), F32),
                pltpu.VMEM((rows, width), BF16),
                pltpu.VMEM((rows, width), BF16),
                dma((4,)), dma((4,)), dma((4,)),
                dma((2,)), dma((2,)), dma((2,)), dma((2,)),
            ],
            compiler_params=pltpu.CompilerParams(
                collective_id=0, has_side_effects=True, vmem_limit_bytes=32 * 2**20),
        )(activations, cotangent, base_weight, skew_param)
        return tuple(pl.pallas_call(
            pair_finish,
            out_shape=outs,
            in_specs=[vmem] * 2,
            out_specs=[pl.BlockSpec(memory_space=pltpu.HBM)] * 2,
            scratch_shapes=[dma((2,))],
            compiler_params=pltpu.CompilerParams(vmem_limit_bytes=32 * 2**20),
        )(*pairs))
    parts = pl.pallas_call(
        functools.partial(exchange, n_dp),
        out_shape=(outs[0],
                   jax.ShapeDtypeStruct((blocks - 1, rows, width), F32),
                   jax.ShapeDtypeStruct((blocks, 5, width, width), BF16),
                   jax.ShapeDtypeStruct((n_dp, tokens, own), BF16),
                   jax.ShapeDtypeStruct((blocks, n_dp, width, tokens), BF16)),
        in_specs=[pl.BlockSpec(memory_space=pltpu.HBM)] * 4,
        out_specs=[vmem] * 5,
        scratch_shapes=[
            pltpu.VMEM((blocks, rows, width), F32),
            pltpu.VMEM((n_dp, blocks, rows, width), wire),
            pltpu.VMEM(cotangent.shape, BF16),
            pltpu.VMEM(cotangent.shape[::-1], BF16),
            pltpu.VMEM(base_weight.shape, BF16),
            pltpu.VMEM((blocks, 2, width, tokens), BF16),
            pltpu.VMEM((blocks, 2, width, tokens), BF16),
            pltpu.VMEM((blocks, 2, width, tokens), F32),
            pltpu.VMEM((blocks, width, tokens), BF16),
            pltpu.VMEM((blocks, width, tokens), BF16),
            pltpu.VMEM((blocks, width, width), BF16),
            pltpu.VMEM((width, width), F32),
            dma((4,)),
            dma((n_dp - 1,)), dma((n_dp - 1,)),
            dma((n_dp - 1,)), dma((n_dp - 1,)),
            dma((blocks,)), dma((blocks,)),
            dma((blocks,)), dma((blocks,)),
            dma((blocks, n_dp - 1)), dma((blocks, n_dp - 1)),
        ],
        compiler_params=pltpu.CompilerParams(
            collective_id=0, has_side_effects=True, vmem_limit_bytes=32 * 2**20),
    )(activations, cotangent, base_weight, skew_param)
    return tuple(pl.pallas_call(
        functools.partial(finish, n_dp),
        out_shape=outs,
        in_specs=[vmem] * 5,
        out_specs=[pl.BlockSpec(memory_space=pltpu.HBM)] * 2,
        scratch_shapes=[pltpu.VMEM((width, width), F32), dma((blocks + 1,))],
        compiler_params=pltpu.CompilerParams(vmem_limit_bytes=32 * 2**20),
    )(*parts))


def solution(mesh):
    return jax.shard_map(
        functools.partial(body, mesh.shape["dp"]),
        mesh=mesh,
        in_specs=(
            P("dp", ("inblk", "outcol")),
            P("dp", "outcol"),
            P("inblk", "outcol"),
            P(("inblk", "outcol"), "dp", None),
        ),
        out_specs=(P("dp", ("inblk", "outcol")), P(("inblk", "outcol"), "dp", None)),
        check_vma=False,
    )
```

```python
import functools

import jax
import jax.numpy as jnp
from jax import lax
from jax.experimental import pallas as pl
from jax.experimental.pallas import tpu as pltpu
from jax.sharding import PartitionSpec as P

F32, BF16 = jnp.float32, jnp.bfloat16
MESH = pl.DeviceIdType.MESH


def mm(left, right):
    return jnp.dot(left, right, preferred_element_type=F32)


def halves(value):
    high = value.astype(BF16)
    return high, (value - high.astype(F32)).astype(BF16)


def mm3(left, right):
    return mm(left[0], right[0]) + (mm(left[0], right[1]) + mm(left[1], right[0]))


def grad_of(n_dp, feat, act_all, block):
    width = feat.shape[2]
    columns = slice(block * width, (block + 1) * width)
    grad = mm(feat[block, 0], act_all[0, :, columns])
    for slot in range(1, n_dp):
        grad = grad + mm(feat[block, slot], act_all[slot, :, columns])
    return grad


def chain(grad, mats, index):
    grad_b = grad.astype(BF16)
    x = mm(mats[index, 0], grad_b) + mm(grad_b, mats[index, 0])
    x_b = x.astype(BF16)
    kx = (x + mm(mats[index, 3], x_b)).astype(BF16)
    lead = 2.0 * grad + x
    dq = (lead + x) + mm(mats[index, 4], x_b)
    dq = dq + mm(lead.astype(BF16), mats[index, 2]) + mm(kx, mats[index, 1])
    return dq.T - dq


def exchange(n_dp, act_hbm, cot_hbm, w_hbm, skew_hbm, ga_ref, gs_ref, mats, act_all, feat,
             skew_own, skew_all, cot_v, cot_t, w_v,
             s1_send, s1_recv, part, y_send, y_recv, rot, dq_v,
             loc, skew_s, skew_r, act_s, act_r, s1_s, s1_r, y_s, y_r, f_s, f_r):
    me, out = lax.axis_index("dp"), lax.axis_index("outcol")
    side, core = lax.div(out, 2), lax.rem(out, 2)
    sib = side * 2 + 1 - core
    far = (1 - side) * 2 + core
    far_sib = (1 - side) * 2 + 1 - core
    blocks, rows, width = skew_own.shape
    peers = [lax.rem(me + step, n_dp) for step in range(1, n_dp)]

    loads = [
        pltpu.make_async_copy(src, dst, loc.at[i])
        for i, (src, dst) in enumerate(
            ((skew_hbm, skew_own), (cot_hbm, cot_v), (w_hbm, w_v), (act_hbm, act_all.at[0]))
        )
    ]
    for load in loads:
        load.start()

    barrier = pltpu.get_barrier_semaphore()
    pl.semaphore_signal(barrier, inc=1, device_id={"outcol": sib}, device_id_type=MESH)
    pl.semaphore_signal(barrier, inc=1, device_id={"outcol": far}, device_id_type=MESH)
    for peer in peers:
        pl.semaphore_signal(barrier, inc=1, device_id={"dp": peer}, device_id_type=MESH)

    def partial_of(owner, block):
        start = pl.multiple_of((owner * blocks + block) * width, width)
        return mm(w_v[pl.ds(start, width), :], cot_t[...])

    def remote(src, dst, send, recv, **where):
        return pltpu.make_async_remote_copy(
            src_ref=src, dst_ref=dst, send_sem=send, recv_sem=recv,
            device_id=where, device_id_type=MESH,
        )

    s1 = [remote(s1_send.at[b], s1_recv.at[b], s1_s.at[b], s1_r.at[b], outcol=sib)
          for b in range(blocks)]
    skews = [remote(skew_all.at[me], skew_all.at[me], skew_s.at[i], skew_r.at[i], dp=peer)
             for i, peer in enumerate(peers)]
    acts = [remote(act_hbm, act_all.at[i + 1], act_s.at[i], act_r.at[i], dp=peer)
            for i, peer in enumerate(peers)]

    loads[0].wait()
    skew_all[me] = skew_own[...].astype(skew_all.dtype)
    loads[1].wait()
    cot_t[...] = cot_v[...].T
    pl.semaphore_wait(barrier, 1 + n_dp)
    for copy in skews:
        copy.start()

    loads[2].wait()
    for block in range(blocks):
        s1_send[block, 0] = partial_of(sib, block).astype(BF16)
        s1_send[block, 1] = partial_of(far_sib, block).astype(BF16)
        s1[block].start()
    for block in range(blocks):
        part[block, 1] = partial_of(far, block)
        part[block, 0] = partial_of(out, block)

    sides = [remote(y_send.at[b], y_recv.at[b], y_s.at[b], y_r.at[b], outcol=far)
             for b in range(blocks)]
    for block in range(blocks):
        s1[block].wait_recv()
        y_send[block] = (part[block, 1] + s1_recv[block, 1].astype(F32)).astype(BF16)
        sides[block].start()
    for copy in acts:
        copy.start()
    eye = (lax.broadcasted_iota(jnp.int32, (width, width), 0)
           == lax.broadcasted_iota(jnp.int32, (width, width), 1)).astype(F32)
    feats = []
    for block in range(blocks):
        sides[block].wait_recv()
        total = part[block, 0] + s1_recv[block, 0].astype(F32) + y_recv[block].astype(F32)
        feat[block, 0] = total.astype(BF16)
        for i, peer in enumerate(peers):
            copy = remote(feat.at[block, 0], feat.at[block, i + 1],
                          f_s.at[block, i], f_r.at[block, i], dp=peer)
            copy.start()
            feats.append(copy)

        if block == 0:
            for copy in skews:
                copy.wait_recv()
        given = skew_all[:, block].reshape(width, width).astype(F32)
        m1 = given - given.T
        m1_h = halves(m1)
        m2 = mm3(m1_h, m1_h)
        m2_h = halves(m2)
        m4 = mm3(m2_h, m2_h)
        k0 = 2.0 * m1 + m2
        k0_h = halves(k0)
        n0 = m2 + m4
        n0_h = halves(n0)
        rot[block] = (eye + ((k0 + n0) + mm3(k0_h, n0_h))).astype(BF16)
        mats[block, 0] = m1_h[0]
        mats[block, 1] = m2_h[0]
        mats[block, 2] = n0_h[0]
        mats[block, 3] = k0_h[0]
        mats[block, 4] = (k0 + m2 + mm(k0_h[0], m2_h[0])).astype(BF16)
    for block in range(blocks):
        ga_ref[:, block * width:(block + 1) * width] = mm(
            rot[block], feat[block, 0]).T.astype(BF16)

    loads[3].wait()
    for copy in acts:
        copy.wait_recv()

    for block in range(blocks):
        for copy in feats[block * (n_dp - 1):(block + 1) * (n_dp - 1)]:
            copy.wait_recv()
        if block < blocks - 1:
            dq_v[...] = chain(grad_of(n_dp, feat, act_all, block), mats, block)
            gs_ref[block] = dq_v[pl.ds(pl.multiple_of(me * rows, rows), rows), :]

    for copy in s1 + skews + acts + sides + feats:
        copy.wait_send()


def finish(n_dp, ga_ref, gs_ref, mats, act_all, feat, ga_out, gs_out, dq_v, sems):
    me = lax.axis_index("dp")
    blocks, rows, width = gs_out.shape
    last = blocks - 1
    writes = [pltpu.make_async_copy(ga_ref, ga_out, sems.at[0])]
    writes += [pltpu.make_async_copy(gs_ref.at[b], gs_out.at[b], sems.at[b + 1])
               for b in range(last)]
    for write in writes:
        write.start()
    dq_v[...] = chain(grad_of(n_dp, feat, act_all, last), mats, last)
    end = pltpu.make_async_copy(dq_v.at[pl.ds(pl.multiple_of(me * rows, rows), rows)],
                                gs_out.at[last], sems.at[blocks])
    end.start()
    for write in writes + [end]:
        write.wait()


def body(n_dp, activations, cotangent, base_weight, skew_param):
    tokens, own = activations.shape
    blocks, rows, width = skew_param.shape
    wire = BF16 if rows % 16 == 0 else F32
    dma = pltpu.SemaphoreType.DMA
    vmem = pl.BlockSpec(memory_space=pltpu.VMEM)
    outs = (jax.ShapeDtypeStruct((tokens, own), BF16),
            jax.ShapeDtypeStruct((blocks, rows, width), F32))
    activations, cotangent, base_weight, skew_param = (
        pltpu.with_memory_space_constraint(each, pltpu.HBM)
        for each in (activations, cotangent, base_weight, skew_param))
    parts = pl.pallas_call(
        functools.partial(exchange, n_dp),
        out_shape=(outs[0],
                   jax.ShapeDtypeStruct((blocks - 1, rows, width), F32),
                   jax.ShapeDtypeStruct((blocks, 5, width, width), BF16),
                   jax.ShapeDtypeStruct((n_dp, tokens, own), BF16),
                   jax.ShapeDtypeStruct((blocks, n_dp, width, tokens), BF16)),
        in_specs=[pl.BlockSpec(memory_space=pltpu.HBM)] * 4,
        out_specs=[vmem] * 5,
        scratch_shapes=[
            pltpu.VMEM((blocks, rows, width), F32),
            pltpu.VMEM((n_dp, blocks, rows, width), wire),
            pltpu.VMEM(cotangent.shape, BF16),
            pltpu.VMEM(cotangent.shape[::-1], BF16),
            pltpu.VMEM(base_weight.shape, BF16),
            pltpu.VMEM((blocks, 2, width, tokens), BF16),
            pltpu.VMEM((blocks, 2, width, tokens), BF16),
            pltpu.VMEM((blocks, 2, width, tokens), F32),
            pltpu.VMEM((blocks, width, tokens), BF16),
            pltpu.VMEM((blocks, width, tokens), BF16),
            pltpu.VMEM((blocks, width, width), BF16),
            pltpu.VMEM((width, width), F32),
            dma((4,)),
            dma((n_dp - 1,)), dma((n_dp - 1,)),
            dma((n_dp - 1,)), dma((n_dp - 1,)),
            dma((blocks,)), dma((blocks,)),
            dma((blocks,)), dma((blocks,)),
            dma((blocks, n_dp - 1)), dma((blocks, n_dp - 1)),
        ],
        compiler_params=pltpu.CompilerParams(
            collective_id=0, has_side_effects=True, vmem_limit_bytes=32 * 2**20),
    )(activations, cotangent, base_weight, skew_param)
    return tuple(pl.pallas_call(
        functools.partial(finish, n_dp),
        out_shape=outs,
        in_specs=[vmem] * 5,
        out_specs=[pl.BlockSpec(memory_space=pltpu.HBM)] * 2,
        scratch_shapes=[pltpu.VMEM((width, width), F32), dma((blocks + 1,))],
        compiler_params=pltpu.CompilerParams(vmem_limit_bytes=32 * 2**20),
    )(*parts))


def solution(mesh):
    return jax.shard_map(
        functools.partial(body, mesh.shape["dp"]),
        mesh=mesh,
        in_specs=(
            P("dp", ("inblk", "outcol")),
            P("dp", "outcol"),
            P("inblk", "outcol"),
            P(("inblk", "outcol"), "dp", None),
        ),
        out_specs=(P("dp", ("inblk", "outcol")), P(("inblk", "outcol"), "dp", None)),
        check_vma=False,
    )
```
